32 devices in a mesh: space: 2 (over x), tm: 16 (over z, y, core).
Axes of the slice: x: 2, y: 2, z: 4, core: 2. Of those that a mesh axis runs over, the one named last changes fastest.
Arguments:
- record: float32 [3072, 8192], P('tm', 'space'), may hold values from -40 to 40
- mode_basis: float32 [21, 48, 48], replicated, may hold values from -0.2 to 1.2
- slow_picks: int32 [21, 32], replicated, may hold values from 0 to 47, all different within a row
- phases: int32 [21], replicated, may hold values from 0 to 3
Outputs:
- residual_record: float32 [3072, 8192], P('tm', 'space')
The draws below stay inside these ranges and needn't reach their ends.
Inputs may be any that keep to these rules, and one draw needn't show every extreme that they name: `slow_picks`: the 32 entries of a row are different.
All inputs are finite; a program needn't handle non-finite values.
Results may differ from the reference program's by a relative error of at most 0.003.
Values may be sent and summed in bfloat16 or wider, within the bound.
No kernel may reach another device: no remote copies, remote signals or barrier semaphores. Data moves between devices by JAX's collectives and lax.ppermute only.
A program may use at most 64 MiB of HBM per device.

```python
import jax
import jax.numpy as jnp
from jax import lax

M = 48
R = 32
WINDOWS = 21
POINTS = 8192
TIMES = 3072


def draw_record(key, part):
    key = jax.random.fold_in(key, 11)
    key_main, key_point, key_snap = jax.random.split(key, 3)
    point_scale = jnp.exp(jax.random.uniform(key_point, (1, POINTS), jnp.float32, jnp.log(0.3), jnp.log(3.0)))
    snap_scale = jnp.exp(jax.random.uniform(key_snap, (TIMES, 1), jnp.float32, jnp.log(0.5), jnp.log(2.0)))
    values = jax.random.truncated_normal(key_main, -5.0, 5.0, (TIMES, POINTS), jnp.float32)
    return values * snap_scale * point_scale


def draw_mode_basis(key, part):
    key = jax.random.fold_in(key, 23)
    noise = 0.06 * jax.random.truncated_normal(key, -3.0, 3.0, (WINDOWS, M, M), jnp.float32)
    return noise + jnp.eye(M, dtype=jnp.float32)[None]


def set_ends(drawn, key, low, top_value):
    index_at = [jax.random.randint(jax.random.fold_in(key, axis), (), 0, length) for axis, length in enumerate(drawn.shape)]
    widest = drawn.shape.index(max(drawn.shape))
    next_to = index_at[:widest] + [(index_at[widest] + 1) % drawn.shape[widest]] + index_at[widest + 1:]
    return drawn.at[tuple(index_at)].set(low).at[tuple(next_to)].set(top_value)


def picks_of(stream_key, rows, count, top, lift):
    sequence = jax.random.permutation(jax.random.fold_in(stream_key, 1), count)
    boost = sequence
    for power in range(3):
        boost = boost * boost // count
    boost = boost * lift // count
    tickets = jax.random.randint(jax.random.fold_in(stream_key, 2), (rows, count), 0, 4096) + boost
    sure = jax.random.permutation(jax.random.fold_in(stream_key, 3), rows)[jnp.arange(count) % rows]
    tickets = jnp.where(jnp.arange(rows)[:, None] == sure[None, :], 1 << 14, tickets)
    score = tickets * count + jnp.arange(count)
    return lax.top_k(score.astype(jnp.int32), top)[1].astype(jnp.int32)


def setup_inputs(seed: int = 0) -> dict:
    keys = jax.random.split(jax.random.key(seed), 5)
    record = draw_record(jax.random.fold_in(keys[4], 71), 0)
    mode_basis = draw_mode_basis(jax.random.fold_in(keys[4], 71), 0)
    slow_picks = picks_of(keys[2], WINDOWS, M, R, 0)
    phases = set_ends(jax.random.randint(keys[3], (WINDOWS,), 0, 4), jax.random.fold_in(keys[3], 1), 0, 3).astype(jnp.int32)
    return dict(record=record, mode_basis=mode_basis, slow_picks=slow_picks, phases=phases)


precise = lax.Precision.HIGHEST

def choose_columns(basis_w, picks_w, gram, points):
    size_m = basis_w.shape[1]
    modes_r = picks_w.shape[1]
    onehot = (picks_w[:, :, None] == jnp.arange(size_m, dtype=jnp.int32)[None, None, :]).astype(jnp.float32)
    chosen = jnp.einsum('wmn,wrn->wmr', basis_w, onehot, precision=precise)
    inner = jnp.einsum('wmn,wnr->wmr', gram, chosen, precision=precise)
    kernel = jnp.einsum('wmr,wms->wrs', chosen, inner, precision=precise) + 1e-05 * jnp.eye(modes_r, dtype=jnp.float32)[None]
    factor = jnp.linalg.cholesky(kernel)
    solved = lax.linalg.triangular_solve(factor, chosen, left_side=False, lower=True, transpose_a=True)
    return solved / jnp.sqrt(jnp.asarray(points, jnp.float32))

def reference(record, mode_basis, slow_picks, phases):
    field = record
    offset_base = 0
    for level in range(3):
        window_count = 4 ** level
        span_len = TIMES // window_count
        stride = span_len // M
        offsets = phases[offset_base:offset_base + window_count] % stride
        indices = (jnp.arange(window_count, dtype=jnp.int32) * span_len)[:, None] + offsets[:, None] + stride * jnp.arange(M, dtype=jnp.int32)[None, :]
        samples = field[indices.reshape(-1)].astype(jnp.bfloat16).reshape(window_count, M, POINTS)
        widened = samples.astype(jnp.float32)
        gram = jnp.einsum('wmp,wnp->wmn', widened, widened, precision=precise) / POINTS
        weights = choose_columns(mode_basis[offset_base:offset_base + window_count], slow_picks[offset_base:offset_base + window_count], gram, POINTS)
        modes = jnp.einsum('wmr,wmp->wrp', weights, widened, precision=precise)
        segments = field.reshape(window_count, span_len, POINTS)
        amplitude = jnp.einsum('wrp,wtp->wrt', modes, segments, precision=precise)
        slow = jnp.einsum('wrt,wrp->wtp', amplitude, modes, precision=precise)
        field = (segments - slow).reshape(TIMES, POINTS)
        offset_base = offset_base + window_count
    return field
```

```python
import functools

import jax
import jax.numpy as jnp
from jax import lax
from jax.experimental import pallas as pl
from jax.experimental.pallas import tpu as pltpu
from jax.sharding import PartitionSpec as P

EPS = 1e-05
HI = lax.Precision.HIGHEST
F32 = jnp.float32
BF16 = jnp.bfloat16
LANES = 128
ROWS = 8
MIB = 1024 * 1024


def dot_nn(a, b, precision=None):
    return lax.dot_general(
        a, b, (((1,), (0,)), ((), ())), precision=precision, preferred_element_type=F32
    )


def dot_nt(a, b, precision=None):
    return lax.dot_general(
        a, b, (((1,), (1,)), ((), ())), precision=precision, preferred_element_type=F32
    )


def dot_tn(a, b, precision=None):
    return lax.dot_general(
        a, b, (((0,), (0,)), ((), ())), precision=precision, preferred_element_type=F32
    )


def split2(x):
    high = x.astype(BF16)
    return high, (x - high.astype(F32)).astype(BF16)


def iota(shape, axis):
    return lax.broadcasted_iota(jnp.int32, shape, axis)


def pick_phase(phases_ref, window, stride):
    phases = phases_ref[...]
    here = iota(phases.shape, 1) == window
    return lax.rem(jnp.sum(jnp.where(here, phases, 0), axis=1, keepdims=True), stride)


def slab_kernel(stride0, x_hbm, slab_ref, sems):
    size = 4
    copies = [
        pltpu.make_async_copy(
            x_hbm.at[pl.ds(stride0 * i, size), :], slab_ref.at[pl.ds(size * i, size), :], sems.at[i]
        )
        for i in range(sems.shape[0])
    ]
    for copy in copies:
        copy.start()
    rows, cols = slab_ref.shape
    used = size * sems.shape[0]
    slab_ref[used:rows] = jnp.zeros((rows - used, cols), F32)
    for copy in copies:
        copy.wait()


def first_kernel(stride0, phases_ref, slab_ref, out_ref, wide_ref):
    rows, cols = slab_ref.shape
    chunks = cols // LANES
    count = out_ref.shape[0] // chunks
    held = wide_ref.shape[0] // chunks
    off = pick_phase(phases_ref, 0, stride0)
    line, place = iota((held, rows), 0), iota((held, rows), 1)
    pick = ((place == 4 * line + off) & (line < count)).astype(BF16)
    wide = 512
    for p in range(cols // wide):
        got = dot_nn(pick, slab_ref[:, p * wide:(p + 1) * wide].astype(BF16))
        for c in range(wide // LANES):
            wide_ref[pl.ds(p * wide // LANES + c, held, stride=chunks), :] = got[
                :, c * LANES:(c + 1) * LANES
            ]
    out_ref[...] = wide_ref[0:count * chunks].astype(BF16)


def local_kernel(strides, phases_ref, x_ref, own0_ref, round_ref, sel_ref, own_ref, wide_ref):
    pos = lax.axis_index("tm")
    steps, cols = x_ref.shape
    chunks = cols // LANES
    size_m = sel_ref.shape[0]
    size0 = own0_ref.shape[0]
    n1 = steps // strides[1]
    held = wide_ref.shape[0] // chunks
    off1 = pick_phase(phases_ref, 1 + lax.div(pos, 4), strides[1])
    off2 = pick_phase(phases_ref, 5 + pos, strides[2])
    line, place = iota((size_m + held, steps), 0), iota((size_m + held, steps), 1)
    second = line >= size_m
    line = jnp.where(second, line - size_m, line)
    target = jnp.where(second, line * strides[1] + off1, line * strides[2] + off2)
    pick = ((place == target) & jnp.logical_not(second & (line >= n1))).astype(BF16)
    parts = 8
    wide = cols // parts
    for p in range(parts):
        at = slice(p * wide, (p + 1) * wide)
        rounded = x_ref[:, at].astype(BF16)
        round_ref[:, at] = rounded
        got = dot_nn(pick, rounded)
        sel_ref[:, at] = got[0:size_m].astype(BF16)
        for c in range(wide // LANES):
            wide_ref[pl.ds(p * wide // LANES + c, held, stride=chunks), :] = got[
                size_m:size_m + held, c * LANES:(c + 1) * LANES
            ]
    own_ref[0:size0] = own0_ref[...]
    own_ref[size0:size0 + n1 * chunks] = wide_ref[0:n1 * chunks].astype(BF16)


def modes_kernel(strides, phases_ref, basis_hbm, picks_ref, bt_ref, bd_ref, bx_ref, basis_ref, sems):
    pos = lax.axis_index("tm")
    modes_r, steps = bx_ref.shape
    size_m = basis_ref.shape[1]
    n0, n1 = steps // strides[0], steps // strides[1]
    windows = [0, 1 + lax.div(pos, 4), 5 + pos]
    copies = [
        pltpu.make_async_copy(basis_hbm.at[windows[level]], basis_ref.at[level], sems.at[level])
        for level in range(3)
    ]
    for copy in copies:
        copy.start()
    lane = iota((1, size_m), 1)

    def placed(width, flips, base):
        order = jnp.zeros((1, size_m), jnp.int32)
        for b, flip in enumerate(flips):
            inside = (lane >= b * width) & (lane < (b + 1) * width)
            order = jnp.where(inside, (base ^ flip) * width + lane - b * width, order)
        return order

    flips0 = [(b // 8) + (b // 4 % 2) * 2 + (0, 4, 12, 8)[b % 4] for b in range(16)]
    flips1 = [(b // 2) + (b % 2) * 2 for b in range(4)]
    orders = [placed(n0, flips0, pos), placed(n1, flips1, lax.rem(pos, 4)), lane]
    for copy in copies:
        copy.wait()
    for level in range(3):
        picks = picks_ref[pl.ds(windows[level], 1), :]
        onehot = (iota((size_m, modes_r), 0) == picks).astype(F32)
        chosen = dot_nn(basis_ref[level], onehot, HI)
        shuffle = (iota((size_m, size_m), 0) == orders[level]).astype(F32)
        bt_ref[level] = dot_tn(chosen, shuffle, HI)
    off2 = pick_phase(phases_ref, windows[2], strides[2])
    place = (iota((size_m, steps), 1) == iota((size_m, steps), 0) * strides[2] + off2)
    bx_ref[...] = dot_nn(bt_ref[2], place.astype(F32), HI)
    bd_ref[...] = jnp.zeros(bd_ref.shape, F32)
    for level in range(3):
        bd_ref[level * modes_r:(level + 1) * modes_r, level * size_m:(level + 1) * size_m] = bt_ref[level]


def unpack(pieces, wide_ref, s_ref, count):
    at = 0
    for piece, first, last in pieces:
        wide_ref[at:at + last - first] = piece[first:last].astype(F32)
        at += last - first
    chunks = s_ref.shape[1] // LANES
    for c in range(chunks):
        s_ref[0:count, c * LANES:(c + 1) * LANES] = wide_ref[
            pl.ds(c, count, stride=chunks), :
        ].astype(BF16)


def gram_kernel(points, size0, sel_ref, *refs):
    near, far, (gram_ref, s_ref, wide_ref, gather_ref) = refs[:4], refs[4:7], refs[7:]
    count, cols = sel_ref.shape
    first = s_ref.shape[0] - 2 * count
    unpack([(piece, size0, piece.shape[0]) for piece in near], wide_ref, gather_ref, count)
    s = gather_ref[0:count]
    gram_ref[...] = dot_nt(s, s) * (1.0 / points)
    s_ref[first:first + count] = s
    s_ref[first + count:first + 2 * count] = sel_ref[...]
    pieces, left = [], first * (cols // LANES)
    for i in range(3):
        for piece, size in ((near[i], size0), (far[i], far[i].shape[0])):
            take = min(size, left)
            if take:
                pieces.append((piece, 0, take))
                left -= take
    unpack(pieces, wide_ref, s_ref, first)


def cross_kernel(points, size0, round_ref, early_ref, gram_ref, bd_ref, bx_ref, far2_ref, near3_ref, far3_ref,
                 w_ref, s_ref, wide_ref):
    r, steps = bx_ref.shape
    count = gram_ref.shape[0]
    first = early_ref.shape[0] - 2 * count
    chunks = early_ref.shape[1] // LANES
    done = (first - count // 2) * chunks - size0
    size = far2_ref.shape[0]
    unpack([(far2_ref, done, size), (near3_ref, 0, size0), (far3_ref, 0, size)], wide_ref, s_ref, count - first)
    s0 = jnp.concatenate([early_ref[0:first], s_ref[...]], axis=0)
    s = jnp.concatenate([s0, early_ref[first:]], axis=0)
    cross = dot_nt(s, jnp.concatenate([round_ref[...], s0], axis=0)) * (1.0 / points)
    b0, b1 = bd_ref[0:r, 0:count], bd_ref[r:2 * r, count:2 * count]
    wx = dot_nn(bd_ref[...], cross[:, 0:steps], HI)
    g0 = dot_nn(bd_ref[0:2 * r, 0:2 * count], cross[0:2 * count, steps:steps + count], HI)
    g1 = dot_nn(b1, gram_ref[...], HI)
    wy = dot_nt(b0, g0, HI)
    at1, at2 = steps, steps + r
    w_ref[:, 0:steps] = wx
    w_ref[0:r, at1:at1 + r] = wy[:, r:2 * r]
    w_ref[r:2 * r, at1:at1 + r] = dot_nt(g1, b1, HI)
    w_ref[2 * r:3 * r, at1:at1 + r] = wy[:, 0:r]
    w_ref[:, at2:at2 + r] = dot_nt(wx, bx_ref[...], HI)


def inverse4(p):
    a, b, d = p[0][0], p[1][0], p[1][1]
    e, f, g, h = p[2][0], p[3][0], p[2][1], p[3][1]
    u, v, w = p[2][2], p[3][2], p[3][3]
    i = 1.0 / (a * d - b * b)
    t00, t01 = (d * e - b * g) * i, (d * f - b * h) * i
    t10, t11 = (a * g - b * e) * i, (a * h - b * f) * i
    s00 = u - (e * t00 + g * t10)
    s01 = v - (e * t01 + g * t11)
    s11 = w - (f * t01 + h * t11)
    j = 1.0 / (s00 * s11 - s01 * s01)
    m22, m23, m33 = s11 * j, -(s01 * j), s00 * j
    y00, y01 = t00 * m22 + t01 * m23, t00 * m23 + t01 * m33
    y10, y11 = t10 * m22 + t11 * m23, t10 * m23 + t11 * m33
    m00 = d * i + (y00 * t00 + y01 * t01)
    m01 = (y00 * t10 + y01 * t11) - b * i
    m11 = a * i + (y10 * t10 + y11 * t11)
    return [
        [m00, m01, -y00, -y01],
        [m01, m11, -y10, -y11],
        [-y00, -y10, m22, m23],
        [-y01, -y11, m23, m33],
    ]


def along_lanes(tile, lane):
    return jnp.broadcast_to(tile[:, lane:lane + 1], tile.shape)


def along_rows(tile, row):
    return jnp.broadcast_to(tile[row:row + 1, :], tile.shape)


def sum4(terms):
    return (terms[0] + terms[1]) + (terms[2] + terms[3])


def eliminate(tiles, at, base, beside=None):
    groups, width = len(tiles), len(tiles[0])
    sub = iota((ROWS, LANES), 0)
    four = range(4)
    tiles = [list(row) for row in tiles]
    cols = [[along_lanes(tiles[g][at], base + j) for g in range(groups)] for j in four]
    pivot = [[along_rows(cols[j][0], i) for j in range(i + 1)] for i in four]
    for k in range(0, groups * ROWS, 4):
        home, first = k // ROWS, k % ROWS
        m = inverse4(pivot)
        if k + 4 < groups * ROWS:
            then, start = (k + 4) // ROWS, (k + 4) % ROWS
            left = [[along_rows(cols[j][then], start + i) for j in four] for i in four]
            diag = [along_lanes(tiles[then][at], base + k + 4 + j) for j in four]
            diag = [[along_rows(diag[j], start + i) for j in range(i + 1)] for i in four]
            mixed = [[sum4([m[a][j] * left[i][j] for j in four]) for i in four] for a in four]
            pivot = [
                [diag[i][j] - sum4([left[i][a] * mixed[a][j] for a in four]) for j in range(i + 1)]
                for i in four
            ]
        rows = [[along_rows(tiles[home][t], first + i) for t in range(width)] for i in four]
        news = [
            [sum4([m[i][j] * rows[j][t] for j in four]) for t in range(width)] for i in four
        ]
        for g in range(groups):
            for t in range(width):
                tile = tiles[g][t] - sum4([cols[j][g] * news[j][t] for j in four])
                if g == home:
                    for i in four:
                        tile = jnp.where(sub == first + i, news[i][t], tile)
                tiles[g][t] = tile
        if k + 4 < groups * ROWS:
            cols = [[along_lanes(tiles[g][at], base + k + 4 + j) for g in range(groups)] for j in four]
        if beside is not None:
            beside(k // 4)
    return tiles


def to_tiles(value):
    return [
        [
            value[g * ROWS:(g + 1) * ROWS, t * LANES:(t + 1) * LANES]
            for t in range(value.shape[1] // LANES)
        ]
        for g in range(value.shape[0] // ROWS)
    ]


def from_tiles(tiles):
    return jnp.concatenate([jnp.concatenate(row, axis=1) for row in tiles], axis=0)


def solve_kernel(w_ref, got_ref, bt_ref, x_ref, early_ref, last_ref, out_hbm, out_ref, z_ref, out_sems):
    r = bt_ref.shape[1]
    count = bt_ref.shape[2]
    steps, cols = x_ref.shape
    first = count - last_ref.shape[0]
    w = w_ref[...] + got_ref[...]
    lanes = w.shape[1]
    b0, b1, b2 = bt_ref[0], bt_ref[1], bt_ref[2]

    def eye_at(base, width):
        return jnp.where(iota((r, width), 0) + base == iota((r, width), 1), EPS, 0.0)

    at1, at2 = steps, steps + r
    a0 = w[0:r]
    k0 = jnp.concatenate([w[2 * r:3 * r, at1:at1 + r], jnp.zeros((r, LANES - r), F32)], axis=1)
    k0 = k0 + eye_at(0, LANES)
    solved = eliminate(to_tiles(jnp.concatenate([a0, k0], axis=1)), lanes // LANES, 0)
    v0 = from_tiles([row[0:lanes // LANES] for row in solved])
    t0 = a0 + EPS * v0
    a1 = w[r:2 * r] - dot_tn(v0[:, at1:at1 + r], t0, HI)
    part2 = w[2 * r:3 * r] - dot_tn(v0[:, at2:at2 + r], t0, HI)
    v1 = from_tiles(eliminate(to_tiles(a1 + eye_at(at1, lanes)), at1 // LANES, at1 % LANES))
    t1 = a1 + EPS * v1
    a2 = part2 - dot_tn(v1[:, at2:at2 + r], t1, HI)
    v0 = v0 - dot_nn(v0[:, at1:at1 + r], v1, HI)
    early = jnp.concatenate(
        [dot_tn(v0[:, 0:steps], b0, HI), dot_tn(v1[:, 0:steps], b1, HI)], axis=1
    )
    early = jnp.concatenate(split2(early), axis=0)
    turn = jnp.concatenate(
        [-dot_tn(v0[:, at2:at2 + r], b0, HI), -dot_tn(v1[:, at2:at2 + r], b1, HI), b2], axis=1
    )
    turn = jnp.concatenate(split2(turn), axis=0)
    parts = r // 4
    wide = cols // parts

    def beside(p):
        at = slice(p * wide, (p + 1) * wide)
        s = jnp.concatenate(
            [early_ref[0:first, at], last_ref[:, at], early_ref[first:, at]], axis=0
        )
        slow = dot_nn(early, s[0:2 * count])
        out_ref[:, at] = x_ref[:, at] - (slow[0:steps] + slow[steps:2 * steps])
        both = dot_nn(turn, s)
        high, low = split2(both[0:r] + both[r:2 * r])
        z_ref[0:r, at] = high
        z_ref[r:2 * r, at] = high
        z_ref[2 * r:3 * r, at] = low

    tile2, lane2 = at2 // LANES, at2 % LANES
    v2 = from_tiles(eliminate(to_tiles(a2 + eye_at(at2, lanes)), tile2, lane2, beside))
    high = v2[:, 0:steps].astype(BF16).astype(F32)
    late = jnp.concatenate([high, v2[:, 0:steps] - high, high], axis=0).T.astype(BF16)
    copies = []
    parts = out_sems.shape[0]
    wide = cols // parts
    for p in range(parts):
        at = slice(p * wide, (p + 1) * wide)
        out_ref[:, at] = out_ref[:, at] - dot_nn(late, z_ref[:, at])
        copy = pltpu.make_async_copy(out_ref.at[:, at], out_hbm.at[:, at], out_sems.at[p])
        copy.start()
        copies.append(copy)
    for copy in copies:
        copy.wait()


def body(record, mode_basis, slow_picks, phases):
    steps, cols = record.shape
    size_m = mode_basis.shape[1]
    modes_r = slow_picks.shape[1]
    groups = lax.axis_size("tm")
    spaces = lax.axis_size("space")
    assert groups == 16 and cols % 512 == 0
    points = cols * spaces
    chunks = cols // LANES
    strides = tuple(steps * groups // (4**level * size_m) for level in range(3))
    n0, n1 = steps // strides[0], steps // strides[1]
    vmem = pl.BlockSpec(memory_space=pltpu.VMEM)
    hbm = pl.BlockSpec(memory_space=pltpu.HBM)

    def cost(flops, size):
        return pl.CostEstimate(flops=flops, bytes_accessed=size, transcendentals=0)

    def limit(size):
        return pltpu.CompilerParams(vmem_limit_bytes=size * MIB)

    def swap(value, bit):
        return lax.ppermute(value, "tm", [(i, i ^ bit) for i in range(groups)])

    def shape(rows, columns, dtype=F32):
        return jax.ShapeDtypeStruct((rows, columns), dtype)

    size0, size1 = n0 * chunks, n1 * chunks
    slab = pl.pallas_call(
        functools.partial(slab_kernel, strides[0]),
        out_shape=shape(16, cols),
        in_specs=[hbm],
        out_specs=vmem,
        scratch_shapes=[pltpu.SemaphoreType.DMA((n0,))],
        compiler_params=limit(53),
        cost_estimate=cost(0, 200000),
        name="sample_slabs",
    )(record)
    own0 = pl.pallas_call(
        functools.partial(first_kernel, strides[0]),
        out_shape=shape(size0, LANES, BF16),
        in_specs=[vmem, vmem],
        out_specs=vmem,
        scratch_shapes=[pltpu.VMEM((16 * chunks, LANES), F32)],
        compiler_params=limit(8),
        cost_estimate=cost(0, 200000),
        name="first_samples",
    )(phases[None], slab)

    z8, z4 = [swap(own0, bit) for bit in (8, 4)]
    rounded, sel, own = pl.pallas_call(
        functools.partial(local_kernel, strides),
        out_shape=(
            shape(steps, cols, BF16), shape(size_m, cols, BF16), shape(size0 + size1, LANES, BF16)
        ),
        in_specs=[vmem] * 3,
        out_specs=(vmem,) * 3,
        scratch_shapes=[pltpu.VMEM((16 * chunks, LANES), F32)],
        compiler_params=limit(12),
        cost_estimate=cost(1000, 1000),
        name="local_samples",
    )(phases[None], record, own0)
    own, z8 = lax.optimization_barrier((own, z8))
    z12 = swap(z8, 4)
    others = [z4, z12, z8]
    side, near = swap(own, 2), swap(own, 1)
    others, rounded, sel = lax.optimization_barrier((others, rounded, sel))
    far = jnp.concatenate(others, axis=0)
    side_far = swap(far, 2)
    far, phases_then = lax.optimization_barrier((far, phases))
    modes = pl.pallas_call(
        functools.partial(modes_kernel, strides),
        out_shape=(
            jax.ShapeDtypeStruct((3, modes_r, size_m), F32),
            shape(3 * modes_r, 3 * size_m),
            shape(modes_r, steps),
        ),
        in_specs=[vmem, hbm, vmem],
        out_specs=(vmem,) * 3,
        scratch_shapes=[
            pltpu.VMEM((3, size_m, size_m), F32),
            pltpu.SemaphoreType.DMA((3,)),
        ],
        compiler_params=limit(4),
        cost_estimate=cost(1000, 1000),
        name="chosen_modes",
    )(phases_then[None], mode_basis, slow_picks)

    side, modes = lax.optimization_barrier((side, modes))
    bt, bd, bx = modes
    near_far, next_side = swap(far, 1), swap(side, 1)
    own_then, side_far, near_far = lax.optimization_barrier((own, side_far, near_far))
    next_far = swap(side_far, 1)
    near = [own_then, side, near, next_side]
    first = 2 * size_m // 3 // 16 * 16
    gram, early = pl.pallas_call(
        functools.partial(gram_kernel, points, size0),
        out_shape=(shape(size_m, size_m), shape(first + 2 * size_m, cols, BF16)),
        in_specs=[vmem] * 8,
        out_specs=(vmem, vmem),
        scratch_shapes=[
            pltpu.VMEM((size_m * chunks, LANES), F32), pltpu.VMEM((size_m, cols), BF16)
        ],
        compiler_params=limit(8),
        cost_estimate=cost(1000, 1000),
        name="level_1_gram",
    )(sel, *near, far, side_far, near_far)
    next_far, gram, early = lax.optimization_barrier((next_far, gram, early))
    w, last = pl.pallas_call(
        functools.partial(cross_kernel, points, size0),
        out_shape=(
            shape(3 * modes_r, steps + 2 * modes_r), shape(size_m - first, cols, BF16)
        ),
        in_specs=[vmem] * 8,
        out_specs=(vmem, vmem),
        scratch_shapes=[pltpu.VMEM(((size_m - first) * chunks, LANES), F32)],
        compiler_params=limit(8),
        cost_estimate=cost(1000000000, 3000000),
        name="cross_products",
    )(rounded, early, gram, bd, bx, near_far, next_side, next_far)

    distance = 1
    other = jnp.zeros_like(w)
    while distance < spaces:
        other = lax.ppermute(w, "space", [(i, i ^ distance) for i in range(spaces)])
        distance *= 2
        if distance < spaces:
            w = w + other

    return pl.pallas_call(
        solve_kernel,
        out_shape=shape(steps, cols),
        in_specs=[vmem] * 6,
        out_specs=hbm,
        scratch_shapes=[
            pltpu.VMEM((steps, cols), F32),
            pltpu.VMEM((3 * modes_r, cols), BF16),
            pltpu.SemaphoreType.DMA((4,)),
        ],
        compiler_params=limit(16),
        cost_estimate=cost(1000000000, 9000000),
        name="remove_slow",
    )(w, other, bt, record, early, last)


def solution(mesh):
    in_specs = (P("tm", "space"), P(), P(), P())
    out_specs = P("tm", "space")
    return jax.shard_map(body, mesh=mesh, in_specs=in_specs, out_specs=out_specs, check_vma=False)
```

```python
import functools

import jax
import jax.numpy as jnp
from jax import lax
from jax.experimental import pallas as pl
from jax.experimental.pallas import tpu as pltpu
from jax.sharding import PartitionSpec as P

EPS = 1e-05
HI = lax.Precision.HIGHEST
F32 = jnp.float32
BF16 = jnp.bfloat16
LANES = 128
ROWS = 8
MIB = 1024 * 1024


def dot_nn(a, b, precision=None):
    return lax.dot_general(
        a, b, (((1,), (0,)), ((), ())), precision=precision, preferred_element_type=F32
    )


def dot_nt(a, b, precision=None):
    return lax.dot_general(
        a, b, (((1,), (1,)), ((), ())), precision=precision, preferred_element_type=F32
    )


def dot_tn(a, b, precision=None):
    return lax.dot_general(
        a, b, (((0,), (0,)), ((), ())), precision=precision, preferred_element_type=F32
    )


def split2(x):
    high = x.astype(BF16)
    return high, (x - high.astype(F32)).astype(BF16)


def iota(shape, axis):
    return lax.broadcasted_iota(jnp.int32, shape, axis)


def pick_phase(phases_ref, window, stride):
    phases = phases_ref[...]
    here = iota(phases.shape, 1) == window
    return lax.rem(jnp.sum(jnp.where(here, phases, 0), axis=1, keepdims=True), stride)


def slab_kernel(stride0, x_hbm, slab_ref, sems):
    size = 4
    copies = [
        pltpu.make_async_copy(
            x_hbm.at[pl.ds(stride0 * i, size), :], slab_ref.at[pl.ds(size * i, size), :], sems.at[i]
        )
        for i in range(sems.shape[0])
    ]
    for copy in copies:
        copy.start()
    rows, cols = slab_ref.shape
    used = size * sems.shape[0]
    slab_ref[used:rows] = jnp.zeros((rows - used, cols), F32)
    for copy in copies:
        copy.wait()


def first_kernel(stride0, phases_ref, slab_ref, out_ref, wide_ref):
    rows, cols = slab_ref.shape
    chunks = cols // LANES
    count = out_ref.shape[0] // chunks
    held = wide_ref.shape[0] // chunks
    off = pick_phase(phases_ref, 0, stride0)
    line, place = iota((held, rows), 0), iota((held, rows), 1)
    pick = ((place == 4 * line + off) & (line < count)).astype(BF16)
    wide = 512
    for p in range(cols // wide):
        got = dot_nn(pick, slab_ref[:, p * wide:(p + 1) * wide].astype(BF16))
        for c in range(wide // LANES):
            wide_ref[pl.ds(p * wide // LANES + c, held, stride=chunks), :] = got[
                :, c * LANES:(c + 1) * LANES
            ]
    out_ref[...] = wide_ref[0:count * chunks].astype(BF16)


def local_kernel(strides, phases_ref, x_ref, own0_ref, round_ref, sel_ref, own_ref, wide_ref):
    pos = lax.axis_index("tm")
    steps, cols = x_ref.shape
    chunks = cols // LANES
    size_m = sel_ref.shape[0]
    size0 = own0_ref.shape[0]
    n1 = steps // strides[1]
    held = wide_ref.shape[0] // chunks
    off1 = pick_phase(phases_ref, 1 + lax.div(pos, 4), strides[1])
    off2 = pick_phase(phases_ref, 5 + pos, strides[2])
    line, place = iota((size_m + held, steps), 0), iota((size_m + held, steps), 1)
    second = line >= size_m
    line = jnp.where(second, line - size_m, line)
    target = jnp.where(second, line * strides[1] + off1, line * strides[2] + off2)
    pick = ((place == target) & jnp.logical_not(second & (line >= n1))).astype(BF16)
    parts = 8
    wide = cols // parts
    for p in range(parts):
        at = slice(p * wide, (p + 1) * wide)
        rounded = x_ref[:, at].astype(BF16)
        round_ref[:, at] = rounded
        got = dot_nn(pick, rounded)
        sel_ref[:, at] = got[0:size_m].astype(BF16)
        for c in range(wide // LANES):
            wide_ref[pl.ds(p * wide // LANES + c, held, stride=chunks), :] = got[
                size_m:size_m + held, c * LANES:(c + 1) * LANES
            ]
    own_ref[0:size0] = own0_ref[...]
    own_ref[size0:size0 + n1 * chunks] = wide_ref[0:n1 * chunks].astype(BF16)


def modes_kernel(strides, phases_ref, basis_hbm, picks_ref, bt_ref, bd_ref, bx_ref, basis_ref, sems):
    pos = lax.axis_index("tm")
    modes_r, steps = bx_ref.shape
    size_m = basis_ref.shape[1]
    n0, n1 = steps // strides[0], steps // strides[1]
    windows = [0, 1 + lax.div(pos, 4), 5 + pos]
    copies = [
        pltpu.make_async_copy(basis_hbm.at[windows[level]], basis_ref.at[level], sems.at[level])
        for level in range(3)
    ]
    for copy in copies:
        copy.start()
    lane = iota((1, size_m), 1)

    def placed(width, flips, base):
        order = jnp.zeros((1, size_m), jnp.int32)
        for b, flip in enumerate(flips):
            inside = (lane >= b * width) & (lane < (b + 1) * width)
            order = jnp.where(inside, (base ^ flip) * width + lane - b * width, order)
        return order

    flips0 = [(b // 8) + (b // 4 % 2) * 2 + (0, 4, 12, 8)[b % 4] for b in range(16)]
    flips1 = [(b // 2) + (b % 2) * 2 for b in range(4)]
    orders = [placed(n0, flips0, pos), placed(n1, flips1, lax.rem(pos, 4)), lane]
    for copy in copies:
        copy.wait()
    for level in range(3):
        picks = picks_ref[pl.ds(windows[level], 1), :]
        onehot = (iota((size_m, modes_r), 0) == picks).astype(F32)
        chosen = dot_nn(basis_ref[level], onehot, HI)
        shuffle = (iota((size_m, size_m), 0) == orders[level]).astype(F32)
        bt_ref[level] = dot_tn(chosen, shuffle, HI)
    off2 = pick_phase(phases_ref, windows[2], strides[2])
    place = (iota((size_m, steps), 1) == iota((size_m, steps), 0) * strides[2] + off2)
    bx_ref[...] = dot_nn(bt_ref[2], place.astype(F32), HI)
    bd_ref[...] = jnp.zeros(bd_ref.shape, F32)
    for level in range(3):
        bd_ref[level * modes_r:(level + 1) * modes_r, level * size_m:(level + 1) * size_m] = bt_ref[level]


def unpack(pieces, wide_ref, s_ref, count):
    at = 0
    for piece, first, last in pieces:
        wide_ref[at:at + last - first] = piece[first:last].astype(F32)
        at += last - first
    chunks = s_ref.shape[1] // LANES
    for c in range(chunks):
        s_ref[0:count, c * LANES:(c + 1) * LANES] = wide_ref[
            pl.ds(c, count, stride=chunks), :
        ].astype(BF16)


def gram_kernel(points, size0, sel_ref, *refs):
    near, far, (gram_ref, s_ref, wide_ref, gather_ref) = refs[:4], refs[4:7], refs[7:]
    count, cols = sel_ref.shape
    first = s_ref.shape[0] - 2 * count
    unpack([(piece, size0, piece.shape[0]) for piece in near], wide_ref, gather_ref, count)
    s = gather_ref[0:count]
    gram_ref[...] = dot_nt(s, s) * (1.0 / points)
    s_ref[first:first + count] = s
    s_ref[first + count:first + 2 * count] = sel_ref[...]
    pieces, left = [], first * (cols // LANES)
    for i in range(3):
        for piece, size in ((near[i], size0), (far[i], far[i].shape[0])):
            take = min(size, left)
            if take:
                pieces.append((piece, 0, take))
                left -= take
    unpack(pieces, wide_ref, s_ref, first)


def cross_kernel(points, size0, round_ref, early_ref, gram_ref, bd_ref, bx_ref, far2_ref, near3_ref, far3_ref,
                 w_ref, s_ref, wide_ref):
    r, steps = bx_ref.shape
    count = gram_ref.shape[0]
    first = early_ref.shape[0] - 2 * count
    chunks = early_ref.shape[1] // LANES
    done = (first - count // 2) * chunks - size0
    size = far2_ref.shape[0]
    unpack([(far2_ref, done, size), (near3_ref, 0, size0), (far3_ref, 0, size)], wide_ref, s_ref, count - first)
    s0 = jnp.concatenate([early_ref[0:first], s_ref[...]], axis=0)
    s = jnp.concatenate([s0, early_ref[first:]], axis=0)
    cross = dot_nt(s, jnp.concatenate([round_ref[...], s0], axis=0)) * (1.0 / points)
    b0, b1 = bd_ref[0:r, 0:count], bd_ref[r:2 * r, count:2 * count]
    wx = dot_nn(bd_ref[...], cross[:, 0:steps], HI)
    g0 = dot_nn(bd_ref[0:2 * r, 0:2 * count], cross[0:2 * count, steps:steps + count], HI)
    g1 = dot_nn(b1, gram_ref[...], HI)
    wy = dot_nt(b0, g0, HI)
    at1, at2 = steps, steps + r
    w_ref[:, 0:steps] = wx
    w_ref[0:r, at1:at1 + r] = wy[:, r:2 * r]
    w_ref[r:2 * r, at1:at1 + r] = dot_nt(g1, b1, HI)
    w_ref[2 * r:3 * r, at1:at1 + r] = wy[:, 0:r]
    w_ref[:, at2:at2 + r] = dot_nt(wx, bx_ref[...], HI)


def inverse4(p):
    a, b, d = p[0][0], p[1][0], p[1][1]
    e, f, g, h = p[2][0], p[3][0], p[2][1], p[3][1]
    u, v, w = p[2][2], p[3][2], p[3][3]
    i = 1.0 / (a * d - b * b)
    t00, t01 = (d * e - b * g) * i, (d * f - b * h) * i
    t10, t11 = (a * g - b * e) * i, (a * h - b * f) * i
    s00 = u - (e * t00 + g * t10)
    s01 = v - (e * t01 + g * t11)
    s11 = w - (f * t01 + h * t11)
    j = 1.0 / (s00 * s11 - s01 * s01)
    m22, m23, m33 = s11 * j, -(s01 * j), s00 * j
    y00, y01 = t00 * m22 + t01 * m23, t00 * m23 + t01 * m33
    y10, y11 = t10 * m22 + t11 * m23, t10 * m23 + t11 * m33
    m00 = d * i + (y00 * t00 + y01 * t01)
    m01 = (y00 * t10 + y01 * t11) - b * i
    m11 = a * i + (y10 * t10 + y11 * t11)
    return [
        [m00, m01, -y00, -y01],
        [m01, m11, -y10, -y11],
        [-y00, -y10, m22, m23],
        [-y01, -y11, m23, m33],
    ]


def along_lanes(tile, lane):
    return jnp.broadcast_to(tile[:, lane:lane + 1], tile.shape)


def along_rows(tile, row):
    return jnp.broadcast_to(tile[row:row + 1, :], tile.shape)


def sum4(terms):
    return (terms[0] + terms[1]) + (terms[2] + terms[3])


def eliminate(tiles, at, base, beside=None):
    groups, width = len(tiles), len(tiles[0])
    sub = iota((ROWS, LANES), 0)
    four = range(4)
    tiles = [list(row) for row in tiles]
    cols = [[along_lanes(tiles[g][at], base + j) for g in range(groups)] for j in four]
    pivot = [[along_rows(cols[j][0], i) for j in range(i + 1)] for i in four]
    for k in range(0, groups * ROWS, 4):
        home, first = k // ROWS, k % ROWS
        m = inverse4(pivot)
        if k + 4 < groups * ROWS:
            then, start = (k + 4) // ROWS, (k + 4) % ROWS
            left = [[along_rows(cols[j][then], start + i) for j in four] for i in four]
            diag = [along_lanes(tiles[then][at], base + k + 4 + j) for j in four]
            diag = [[along_rows(diag[j], start + i) for j in range(i + 1)] for i in four]
            mixed = [[sum4([m[a][j] * left[i][j] for j in four]) for i in four] for a in four]
            pivot = [
                [diag[i][j] - sum4([left[i][a] * mixed[a][j] for a in four]) for j in range(i + 1)]
                for i in four
            ]
        rows = [[along_rows(tiles[home][t], first + i) for t in range(width)] for i in four]
        news = [
            [sum4([m[i][j] * rows[j][t] for j in four]) for t in range(width)] for i in four
        ]
        for g in range(groups):
            for t in range(width):
                tile = tiles[g][t] - sum4([cols[j][g] * news[j][t] for j in four])
                if g == home:
                    for i in four:
                        tile = jnp.where(sub == first + i, news[i][t], tile)
                tiles[g][t] = tile
        if k + 4 < groups * ROWS:
            cols = [[along_lanes(tiles[g][at], base + k + 4 + j) for g in range(groups)] for j in four]
        if beside is not None:
            beside(k // 4)
    return tiles


def to_tiles(value):
    return [
        [
            value[g * ROWS:(g + 1) * ROWS, t * LANES:(t + 1) * LANES]
            for t in range(value.shape[1] // LANES)
        ]
        for g in range(value.shape[0] // ROWS)
    ]


def from_tiles(tiles):
    return jnp.concatenate([jnp.concatenate(row, axis=1) for row in tiles], axis=0)


def solve_kernel(w_ref, got_ref, bt_ref, x_ref, early_ref, last_ref, out_hbm, out_ref, z1_ref, z2_ref, out_sems):
    r = bt_ref.shape[1]
    count = bt_ref.shape[2]
    steps, cols = x_ref.shape
    first = count - last_ref.shape[0]
    w = w_ref[...] + got_ref[...]
    lanes = w.shape[1]
    b0, b1, b2 = bt_ref[0], bt_ref[1], bt_ref[2]

    def eye_at(base, width):
        return jnp.where(iota((r, width), 0) + base == iota((r, width), 1), EPS, 0.0)

    at1, at2 = steps, steps + r
    assert at1 // LANES == (at2 + r - 1) // LANES
    a0 = w[0:r]
    tile1, lane1 = at1 // LANES, at1 % LANES
    tile2, lane2 = at2 // LANES, at2 % LANES
    k0 = w[2 * r:3 * r] + eye_at(at1, lanes)
    solved = eliminate(
        to_tiles(jnp.concatenate([a0, k0[:, tile1 * LANES:(tile1 + 1) * LANES]], axis=1)),
        lanes // LANES, lane1,
    )
    v0 = from_tiles([row[0:lanes // LANES] for row in solved])
    t0 = a0 + EPS * v0
    a1 = w[r:2 * r] - dot_tn(v0[:, at1:at1 + r], t0, HI)
    part2 = w[2 * r:3 * r] - dot_tn(v0[:, at2:at2 + r], t0, HI)
    parts = r // 4
    wide = cols // parts

    def samples_at(at):
        return jnp.concatenate(
            [early_ref[0:first, at], last_ref[:, at], early_ref[first:, at]], axis=0
        )

    def keep(ref, at, both):
        high, low = split2(both[0:r] + both[r:2 * r])
        ref[0:r, at] = high
        ref[r:2 * r, at] = high
        ref[2 * r:3 * r, at] = low

    def turned(value):
        high = value.astype(BF16).astype(F32)
        return jnp.concatenate([high, value - high, high], axis=0).T.astype(BF16)

    v01 = v0[:, at1:at1 + r]
    coef0 = jnp.concatenate(split2(dot_tn(v0[:, 0:steps], b0, HI)), axis=0)
    turn1 = jnp.concatenate([-dot_tn(v01, b0, HI), b1], axis=1)
    turn1 = jnp.concatenate(split2(turn1), axis=0)

    def beside1(p):
        at = slice(p * wide, (p + 1) * wide)
        s = samples_at(at)
        slow = dot_nn(coef0, s[0:count])
        out_ref[:, at] = x_ref[:, at] - (slow[0:steps] + slow[steps:2 * steps])
        keep(z1_ref, at, dot_nn(turn1, s[0:2 * count]))

    v1 = from_tiles(eliminate(to_tiles(a1 + eye_at(at1, lanes)), tile1, lane1, beside1))
    t1 = a1 + EPS * v1
    a2 = part2 - dot_tn(v1[:, at2:at2 + r], t1, HI)
    v12 = v1[:, at2:at2 + r]
    v02 = v0[:, at2:at2 + r] - dot_nn(v01, v12, HI)
    late1 = turned(v1[:, 0:steps])
    turn2 = jnp.concatenate([-dot_tn(v02, b0, HI), -dot_tn(v12, b1, HI), b2], axis=1)
    turn2 = jnp.concatenate(split2(turn2), axis=0)

    def beside2(p):
        at = slice(p * wide, (p + 1) * wide)
        out_ref[:, at] = out_ref[:, at] - dot_nn(late1, z1_ref[:, at])
        keep(z2_ref, at, dot_nn(turn2, samples_at(at)))

    v2 = from_tiles(eliminate(to_tiles(a2 + eye_at(at2, lanes)), tile2, lane2, beside2))
    late2 = turned(v2[:, 0:steps])
    copies = []
    parts = out_sems.shape[0]
    wide = cols // parts
    for p in range(parts):
        at = slice(p * wide, (p + 1) * wide)
        out_ref[:, at] = out_ref[:, at] - dot_nn(late2, z2_ref[:, at])
        copy = pltpu.make_async_copy(out_ref.at[:, at], out_hbm.at[:, at], out_sems.at[p])
        copy.start()
        copies.append(copy)
    for copy in copies:
        copy.wait()


def body(record, mode_basis, slow_picks, phases):
    steps, cols = record.shape
    size_m = mode_basis.shape[1]
    modes_r = slow_picks.shape[1]
    groups = lax.axis_size("tm")
    spaces = lax.axis_size("space")
    assert groups == 16 and cols % 512 == 0
    points = cols * spaces
    chunks = cols // LANES
    strides = tuple(steps * groups // (4**level * size_m) for level in range(3))
    n0, n1 = steps // strides[0], steps // strides[1]
    vmem = pl.BlockSpec(memory_space=pltpu.VMEM)
    hbm = pl.BlockSpec(memory_space=pltpu.HBM)

    def cost(flops, size):
        return pl.CostEstimate(flops=flops, bytes_accessed=size, transcendentals=0)

    def limit(size):
        return pltpu.CompilerParams(vmem_limit_bytes=size * MIB)

    def swap(value, bit):
        return lax.ppermute(value, "tm", [(i, i ^ bit) for i in range(groups)])

    def shape(rows, columns, dtype=F32):
        return jax.ShapeDtypeStruct((rows, columns), dtype)

    size0, size1 = n0 * chunks, n1 * chunks
    slab = pl.pallas_call(
        functools.partial(slab_kernel, strides[0]),
        out_shape=shape(16, cols),
        in_specs=[hbm],
        out_specs=vmem,
        scratch_shapes=[pltpu.SemaphoreType.DMA((n0,))],
        compiler_params=limit(53),
        cost_estimate=cost(0, 200000),
        name="sample_slabs",
    )(record)
    own0 = pl.pallas_call(
        functools.partial(first_kernel, strides[0]),
        out_shape=shape(size0, LANES, BF16),
        in_specs=[vmem, vmem],
        out_specs=vmem,
        scratch_shapes=[pltpu.VMEM((16 * chunks, LANES), F32)],
        compiler_params=limit(8),
        cost_estimate=cost(0, 200000),
        name="first_samples",
    )(phases[None], slab)

    z8, z12, z4 = [swap(own0, bit) for bit in (8, 12, 4)]
    others = [z4, z12, z8]
    rounded, sel, own = pl.pallas_call(
        functools.partial(local_kernel, strides),
        out_shape=(
            shape(steps, cols, BF16), shape(size_m, cols, BF16), shape(size0 + size1, LANES, BF16)
        ),
        in_specs=[vmem] * 3,
        out_specs=(vmem,) * 3,
        scratch_shapes=[pltpu.VMEM((16 * chunks, LANES), F32)],
        compiler_params=limit(12),
        cost_estimate=cost(1000, 1000),
        name="local_samples",
    )(phases[None], record, own0)
    side, near = swap(own, 2), swap(own, 1)
    others, rounded, sel = lax.optimization_barrier((others, rounded, sel))
    far = jnp.concatenate(others, axis=0)
    side_far = swap(far, 2)
    far, phases_then = lax.optimization_barrier((far, phases))
    modes = pl.pallas_call(
        functools.partial(modes_kernel, strides),
        out_shape=(
            jax.ShapeDtypeStruct((3, modes_r, size_m), F32),
            shape(3 * modes_r, 3 * size_m),
            shape(modes_r, steps),
        ),
        in_specs=[vmem, hbm, vmem],
        out_specs=(vmem,) * 3,
        scratch_shapes=[
            pltpu.VMEM((3, size_m, size_m), F32),
            pltpu.SemaphoreType.DMA((3,)),
        ],
        compiler_params=limit(4),
        cost_estimate=cost(1000, 1000),
        name="chosen_modes",
    )(phases_then[None], mode_basis, slow_picks)

    side, modes = lax.optimization_barrier((side, modes))
    bt, bd, bx = modes
    near_far, next_side = swap(far, 1), swap(side, 1)
    own_then, side_far, near_far = lax.optimization_barrier((own, side_far, near_far))
    next_far = swap(side_far, 1)
    near = [own_then, side, near, next_side]
    first = 2 * size_m // 3 // 16 * 16
    gram, early = pl.pallas_call(
        functools.partial(gram_kernel, points, size0),
        out_shape=(shape(size_m, size_m), shape(first + 2 * size_m, cols, BF16)),
        in_specs=[vmem] * 8,
        out_specs=(vmem, vmem),
        scratch_shapes=[
            pltpu.VMEM((size_m * chunks, LANES), F32), pltpu.VMEM((size_m, cols), BF16)
        ],
        compiler_params=limit(8),
        cost_estimate=cost(1000, 1000),
        name="level_1_gram",
    )(sel, *near, far, side_far, near_far)
    next_far, gram, early = lax.optimization_barrier((next_far, gram, early))
    w, last = pl.pallas_call(
        functools.partial(cross_kernel, points, size0),
        out_shape=(
            shape(3 * modes_r, steps + 2 * modes_r), shape(size_m - first, cols, BF16)
        ),
        in_specs=[vmem] * 8,
        out_specs=(vmem, vmem),
        scratch_shapes=[pltpu.VMEM(((size_m - first) * chunks, LANES), F32)],
        compiler_params=limit(8),
        cost_estimate=cost(1000000000, 3000000),
        name="cross_products",
    )(rounded, early, gram, bd, bx, near_far, next_side, next_far)

    distance = 1
    other = jnp.zeros_like(w)
    while distance < spaces:
        other = lax.ppermute(w, "space", [(i, i ^ distance) for i in range(spaces)])
        distance *= 2
        if distance < spaces:
            w = w + other

    return pl.pallas_call(
        solve_kernel,
        out_shape=shape(steps, cols),
        in_specs=[vmem] * 6,
        out_specs=hbm,
        scratch_shapes=[
            pltpu.VMEM((steps, cols), F32),
            pltpu.VMEM((3 * modes_r, cols), BF16),
            pltpu.VMEM((3 * modes_r, cols), BF16),
            pltpu.SemaphoreType.DMA((8,)),
        ],
        compiler_params=limit(16),
        cost_estimate=cost(1000000000, 9000000),
        name="remove_slow",
    )(w, other, bt, record, early, last)


def solution(mesh):
    in_specs = (P("tm", "space"), P(), P(), P())
    out_specs = P("tm", "space")
    return jax.shard_map(body, mesh=mesh, in_specs=in_specs, out_specs=out_specs, check_vma=False)
```

```python
import functools

import jax
import jax.numpy as jnp
from jax import lax
from jax.experimental import pallas as pl
from jax.experimental.pallas import tpu as pltpu
from jax.sharding import PartitionSpec as P

EPS = 1e-05
HI = lax.Precision.HIGHEST
F32 = jnp.float32
BF16 = jnp.bfloat16
LANES = 128
ROWS = 8
MIB = 1024 * 1024


def dot_nn(a, b, precision=None):
    return lax.dot_general(
        a, b, (((1,), (0,)), ((), ())), precision=precision, preferred_element_type=F32
    )


def dot_nt(a, b, precision=None):
    return lax.dot_general(
        a, b, (((1,), (1,)), ((), ())), precision=precision, preferred_element_type=F32
    )


def dot_tn(a, b, precision=None):
    return lax.dot_general(
        a, b, (((0,), (0,)), ((), ())), precision=precision, preferred_element_type=F32
    )


def split2(x):
    high = x.astype(BF16)
    return high, (x - high.astype(F32)).astype(BF16)


def split3(x):
    high = x.astype(BF16)
    rest = x - high.astype(F32)
    middle = rest.astype(BF16)
    return high, middle, (rest - middle.astype(F32)).astype(BF16)


def dot_six(a, b):
    m = a.shape[0]
    a0, a1, a2 = split3(a)
    b0, b1, b2 = split3(b)
    p0 = dot_nn(jnp.concatenate([a0, a1, a2], axis=0), b0)
    p1 = dot_nn(jnp.concatenate([a0, a1], axis=0), b1)
    p2 = dot_nn(a0, b2)
    small = (p0[2 * m:3 * m] + p1[m:2 * m]) + p2
    return (small + (p0[m:2 * m] + p1[0:m])) + p0[0:m]


def iota(shape, axis):
    return lax.broadcasted_iota(jnp.int32, shape, axis)


def pick_phase(phases_ref, window, stride):
    phases = phases_ref[...]
    here = iota(phases.shape, 1) == window
    return lax.rem(jnp.sum(jnp.where(here, phases, 0), axis=1, keepdims=True), stride)


def slab_kernel(stride0, x_hbm, slab_ref, sems):
    size = 4
    copies = [
        pltpu.make_async_copy(
            x_hbm.at[pl.ds(stride0 * i, size), :], slab_ref.at[pl.ds(size * i, size), :], sems.at[i]
        )
        for i in range(sems.shape[0])
    ]
    for copy in copies:
        copy.start(priority=1)
    rows, cols = slab_ref.shape
    used = size * sems.shape[0]
    slab_ref[used:rows] = jnp.zeros((rows - used, cols), F32)
    for copy in copies:
        copy.wait()


def first_kernel(stride0, phases_ref, slab_ref, out_ref, wide_ref):
    rows, cols = slab_ref.shape
    chunks = cols // LANES
    count = out_ref.shape[0] // chunks
    held = wide_ref.shape[0] // chunks
    off = pick_phase(phases_ref, 0, stride0)
    line, place = iota((held, rows), 0), iota((held, rows), 1)
    pick = ((place == 4 * line + off) & (line < count)).astype(BF16)
    wide = 512
    for p in range(cols // wide):
        got = dot_nn(pick, slab_ref[:, p * wide:(p + 1) * wide].astype(BF16))
        for c in range(wide // LANES):
            wide_ref[pl.ds(p * wide // LANES + c, held, stride=chunks), :] = got[
                :, c * LANES:(c + 1) * LANES
            ]
    out_ref[...] = wide_ref[0:count * chunks].astype(BF16)


def local_kernel(strides, phases_ref, x_ref, own0_ref, round_ref, sel_ref, own_ref, wide_ref):
    pos = lax.axis_index("tm")
    steps, cols = x_ref.shape
    chunks = cols // LANES
    size_m = sel_ref.shape[0]
    size0 = own0_ref.shape[0]
    n1 = steps // strides[1]
    held = wide_ref.shape[0] // chunks
    off1 = pick_phase(phases_ref, 1 + lax.div(pos, 4), strides[1])
    off2 = pick_phase(phases_ref, 5 + pos, strides[2])
    line, place = iota((size_m + held, steps), 0), iota((size_m + held, steps), 1)
    second = line >= size_m
    line = jnp.where(second, line - size_m, line)
    target = jnp.where(second, line * strides[1] + off1, line * strides[2] + off2)
    pick = ((place == target) & jnp.logical_not(second & (line >= n1))).astype(BF16)
    parts = 8
    wide = cols // parts
    for p in range(parts):
        at = slice(p * wide, (p + 1) * wide)
        rounded = x_ref[:, at].astype(BF16)
        round_ref[:, at] = rounded
        got = dot_nn(pick, rounded)
        sel_ref[:, at] = got[0:size_m].astype(BF16)
        for c in range(wide // LANES):
            wide_ref[pl.ds(p * wide // LANES + c, held, stride=chunks), :] = got[
                size_m:size_m + held, c * LANES:(c + 1) * LANES
            ]
    own_ref[0:size0] = own0_ref[...]
    own_ref[size0:size0 + n1 * chunks] = wide_ref[0:n1 * chunks].astype(BF16)


def modes_kernel(strides, phases_ref, basis_hbm, picks_ref, bt_ref, bd_ref, bx_ref, basis_ref, sems):
    pos = lax.axis_index("tm")
    modes_r, steps = bx_ref.shape
    size_m = basis_ref.shape[1]
    n0, n1 = steps // strides[0], steps // strides[1]
    windows = [0, 1 + lax.div(pos, 4), 5 + pos]
    copies = [
        pltpu.make_async_copy(basis_hbm.at[windows[level]], basis_ref.at[level], sems.at[level])
        for level in range(3)
    ]
    for copy in copies:
        copy.start()
    lane = iota((1, size_m), 1)

    def placed(width, flips, base):
        order = jnp.zeros((1, size_m), jnp.int32)
        for b, flip in enumerate(flips):
            inside = (lane >= b * width) & (lane < (b + 1) * width)
            order = jnp.where(inside, (base ^ flip) * width + lane - b * width, order)
        return order

    flips0 = [(b // 8) + (b // 4 % 2) * 2 + (0, 4, 12, 8)[b % 4] for b in range(16)]
    flips1 = [(b // 2) + (b % 2) * 2 for b in range(4)]
    orders = [placed(n0, flips0, pos), placed(n1, flips1, lax.rem(pos, 4)), lane]
    for copy in copies:
        copy.wait()
    for level in range(3):
        picks = picks_ref[pl.ds(windows[level], 1), :]
        onehot = (iota((size_m, modes_r), 0) == picks).astype(F32)
        chosen = dot_nn(basis_ref[level], onehot, HI)
        shuffle = (iota((size_m, size_m), 0) == orders[level]).astype(F32)
        bt_ref[level] = dot_tn(chosen, shuffle, HI)
    off2 = pick_phase(phases_ref, windows[2], strides[2])
    place = (iota((size_m, steps), 1) == iota((size_m, steps), 0) * strides[2] + off2)
    bx_ref[...] = dot_nn(bt_ref[2], place.astype(F32), HI)
    bd_ref[...] = jnp.zeros(bd_ref.shape, F32)
    for level in range(3):
        bd_ref[level * modes_r:(level + 1) * modes_r, level * size_m:(level + 1) * size_m] = bt_ref[level]


def unpack(pieces, wide_ref, s_ref, count):
    at = 0
    for piece, first, last in pieces:
        wide_ref[at:at + last - first] = piece[first:last].astype(F32)
        at += last - first
    chunks = s_ref.shape[1] // LANES
    for c in range(chunks):
        s_ref[0:count, c * LANES:(c + 1) * LANES] = wide_ref[
            pl.ds(c, count, stride=chunks), :
        ].astype(BF16)


def gram_kernel(points, size0, sel_ref, *refs):
    near, far, (gram_ref, s_ref, wide_ref, gather_ref) = refs[:4], refs[4:7], refs[7:]
    count, cols = sel_ref.shape
    first = s_ref.shape[0] - 2 * count
    unpack([(piece, size0, piece.shape[0]) for piece in near], wide_ref, gather_ref, count)
    s = gather_ref[0:count]
    gram_ref[...] = dot_nt(s, s) * (1.0 / points)
    s_ref[first:first + count] = s
    s_ref[first + count:first + 2 * count] = sel_ref[...]
    pieces, left = [], first * (cols // LANES)
    for i in range(3):
        for piece, size in ((near[i], size0), (far[i], far[i].shape[0])):
            take = min(size, left)
            if take:
                pieces.append((piece, 0, take))
                left -= take
    unpack(pieces, wide_ref, s_ref, first)


def cross_kernel(points, size0, round_ref, early_ref, gram_ref, bd_ref, bx_ref, far2_ref, near3_ref, far3_ref,
                 w_ref, s_ref, wide_ref):
    r, steps = bx_ref.shape
    count = gram_ref.shape[0]
    first = early_ref.shape[0] - 2 * count
    chunks = early_ref.shape[1] // LANES
    done = (first - count // 2) * chunks - size0
    size = far2_ref.shape[0]
    unpack([(far2_ref, done, size), (near3_ref, 0, size0), (far3_ref, 0, size)], wide_ref, s_ref, count - first)
    s0 = jnp.concatenate([early_ref[0:first], s_ref[...]], axis=0)
    s = jnp.concatenate([s0, early_ref[first:]], axis=0)
    cross = dot_nt(s, jnp.concatenate([round_ref[...], s0], axis=0)) * (1.0 / points)
    b0, b1 = bd_ref[0:r, 0:count], bd_ref[r:2 * r, count:2 * count]
    wx = dot_six(bd_ref[...], cross[:, 0:steps])
    g0 = dot_nn(bd_ref[0:2 * r, 0:2 * count], cross[0:2 * count, steps:steps + count], HI)
    g1 = dot_nn(b1, gram_ref[...], HI)
    wy = dot_nt(b0, g0, HI)
    at1, at2 = steps, steps + r
    w_ref[:, 0:steps] = wx
    w_ref[0:r, at1:at1 + r] = wy[:, r:2 * r]
    w_ref[r:2 * r, at1:at1 + r] = dot_nt(g1, b1, HI)
    w_ref[2 * r:3 * r, at1:at1 + r] = wy[:, 0:r]
    w_ref[:, at2:at2 + r] = dot_nt(wx, bx_ref[...], HI)


def inverse4(p):
    a, b, d = p[0][0], p[1][0], p[1][1]
    e, f, g, h = p[2][0], p[3][0], p[2][1], p[3][1]
    u, v, w = p[2][2], p[3][2], p[3][3]
    i = 1.0 / (a * d - b * b)
    t00, t01 = (d * e - b * g) * i, (d * f - b * h) * i
    t10, t11 = (a * g - b * e) * i, (a * h - b * f) * i
    s00 = u - (e * t00 + g * t10)
    s01 = v - (e * t01 + g * t11)
    s11 = w - (f * t01 + h * t11)
    j = 1.0 / (s00 * s11 - s01 * s01)
    m22, m23, m33 = s11 * j, -(s01 * j), s00 * j
    y00, y01 = t00 * m22 + t01 * m23, t00 * m23 + t01 * m33
    y10, y11 = t10 * m22 + t11 * m23, t10 * m23 + t11 * m33
    m00 = d * i + (y00 * t00 + y01 * t01)
    m01 = (y00 * t10 + y01 * t11) - b * i
    m11 = a * i + (y10 * t10 + y11 * t11)
    return [
        [m00, m01, -y00, -y01],
        [m01, m11, -y10, -y11],
        [-y00, -y10, m22, m23],
        [-y01, -y11, m23, m33],
    ]


def along_lanes(tile, lane):
    return jnp.broadcast_to(tile[:, lane:lane + 1], tile.shape)


def along_rows(tile, row):
    return jnp.broadcast_to(tile[row:row + 1, :], tile.shape)


def sum4(terms):
    return (terms[0] + terms[1]) + (terms[2] + terms[3])


def eliminate(tiles, at, base, beside=None):
    groups, width = len(tiles), len(tiles[0])
    sub = iota((ROWS, LANES), 0)
    four = range(4)
    tiles = [list(row) for row in tiles]
    cols = [[along_lanes(tiles[g][at], base + j) for g in range(groups)] for j in four]
    pivot = [[along_rows(cols[j][0], i) for j in range(i + 1)] for i in four]
    for k in range(0, groups * ROWS, 4):
        home, first = k // ROWS, k % ROWS
        m = inverse4(pivot)
        if k + 4 < groups * ROWS:
            then, start = (k + 4) // ROWS, (k + 4) % ROWS
            left = [[along_rows(cols[j][then], start + i) for j in four] for i in four]
            diag = [along_lanes(tiles[then][at], base + k + 4 + j) for j in four]
            diag = [[along_rows(diag[j], start + i) for j in range(i + 1)] for i in four]
            mixed = [[sum4([m[a][j] * left[i][j] for j in four]) for i in four] for a in four]
            pivot = [
                [diag[i][j] - sum4([left[i][a] * mixed[a][j] for a in four]) for j in range(i + 1)]
                for i in four
            ]
        rows = [[along_rows(tiles[home][t], first + i) for t in range(width)] for i in four]
        news = [
            [sum4([m[i][j] * rows[j][t] for j in four]) for t in range(width)] for i in four
        ]
        for g in range(groups):
            for t in range(width):
                tile = tiles[g][t] - sum4([cols[j][g] * news[j][t] for j in four])
                if g == home:
                    for i in four:
                        tile = jnp.where(sub == first + i, news[i][t], tile)
                tiles[g][t] = tile
        if k + 4 < groups * ROWS:
            cols = [[along_lanes(tiles[g][at], base + k + 4 + j) for g in range(groups)] for j in four]
        if beside is not None and k % 8 == 0:
            beside(k // 8)
    return tiles


def to_tiles(value):
    return [
        [
            value[g * ROWS:(g + 1) * ROWS, t * LANES:(t + 1) * LANES]
            for t in range(value.shape[1] // LANES)
        ]
        for g in range(value.shape[0] // ROWS)
    ]


def from_tiles(tiles):
    return jnp.concatenate([jnp.concatenate(row, axis=1) for row in tiles], axis=0)


def solve_kernel(w_ref, got_ref, bt_ref, x_ref, early_ref, last_ref, out_hbm, out_ref, z_ref, out_sems):
    r = bt_ref.shape[1]
    count = bt_ref.shape[2]
    steps, cols = x_ref.shape
    first = count - last_ref.shape[0]
    w = w_ref[...] + got_ref[...]
    lanes = w.shape[1]
    b0, b1, b2 = bt_ref[0], bt_ref[1], bt_ref[2]

    def eye_at(base, width):
        return jnp.where(iota((r, width), 0) + base == iota((r, width), 1), EPS, 0.0)

    at1, at2 = steps, steps + r
    assert at1 // LANES == (at2 + r - 1) // LANES
    a0 = w[0:r]
    tile1, lane1 = at1 // LANES, at1 % LANES
    tile2, lane2 = at2 // LANES, at2 % LANES
    k0 = w[2 * r:3 * r] + eye_at(at1, lanes)
    solved = eliminate(
        to_tiles(jnp.concatenate([a0, k0[:, tile1 * LANES:(tile1 + 1) * LANES]], axis=1)),
        lanes // LANES, lane1,
    )
    v0 = from_tiles([row[0:lanes // LANES] for row in solved])
    t0 = a0 + EPS * v0
    a1 = w[r:2 * r] - dot_tn(v0[:, at1:at1 + r], t0, HI)
    part2 = w[2 * r:3 * r] - dot_tn(v0[:, at2:at2 + r], t0, HI)
    v1 = from_tiles(eliminate(to_tiles(a1 + eye_at(at1, lanes)), tile1, lane1))
    t1 = a1 + EPS * v1
    a2 = part2 - dot_tn(v1[:, at2:at2 + r], t1, HI)
    v0 = v0 - dot_nn(v0[:, at1:at1 + r], v1, HI)
    early = jnp.concatenate(
        [dot_tn(v0[:, 0:steps], b0, HI), dot_tn(v1[:, 0:steps], b1, HI)], axis=1
    )
    early = jnp.concatenate(split2(early), axis=0)
    turn = jnp.concatenate(
        [-dot_tn(v0[:, at2:at2 + r], b0, HI), -dot_tn(v1[:, at2:at2 + r], b1, HI), b2], axis=1
    )
    turn = jnp.concatenate(split2(turn), axis=0)
    parts = r // 8
    wide = cols // parts

    def beside(p):
        at = slice(p * wide, (p + 1) * wide)
        s = jnp.concatenate(
            [early_ref[0:first, at], last_ref[:, at], early_ref[first:, at]], axis=0
        )
        slow = dot_nn(early, s[0:2 * count])
        out_ref[:, at] = x_ref[:, at] - (slow[0:steps] + slow[steps:2 * steps])
        both = dot_nn(turn, s)
        high, low = split2(both[0:r] + both[r:2 * r])
        z_ref[0:r, at] = high
        z_ref[r:2 * r, at] = high
        z_ref[2 * r:3 * r, at] = low

    v2 = from_tiles(eliminate(to_tiles(a2 + eye_at(at2, lanes)), tile2, lane2, beside))
    high = v2[:, 0:steps].astype(BF16).astype(F32)
    late = jnp.concatenate([high, v2[:, 0:steps] - high, high], axis=0).T.astype(BF16)
    copies = []
    parts = out_sems.shape[0]
    wide = cols // parts
    for p in range(parts):
        at = slice(p * wide, (p + 1) * wide)
        out_ref[:, at] = out_ref[:, at] - dot_nn(late, z_ref[:, at])
        copy = pltpu.make_async_copy(out_ref.at[:, at], out_hbm.at[:, at], out_sems.at[p])
        copy.start()
        copies.append(copy)
    for copy in copies:
        copy.wait()


def body(record, mode_basis, slow_picks, phases):
    steps, cols = record.shape
    size_m = mode_basis.shape[1]
    modes_r = slow_picks.shape[1]
    groups = lax.axis_size("tm")
    spaces = lax.axis_size("space")
    assert groups == 16 and cols % 512 == 0
    points = cols * spaces
    chunks = cols // LANES
    strides = tuple(steps * groups // (4**level * size_m) for level in range(3))
    n0, n1 = steps // strides[0], steps // strides[1]
    vmem = pl.BlockSpec(memory_space=pltpu.VMEM)
    hbm = pl.BlockSpec(memory_space=pltpu.HBM)

    def cost(flops, size):
        return pl.CostEstimate(flops=flops, bytes_accessed=size, transcendentals=0)

    def limit(size):
        return pltpu.CompilerParams(vmem_limit_bytes=size * MIB)

    def swap(value, bit):
        return lax.ppermute(value, "tm", [(i, i ^ bit) for i in range(groups)])

    def shape(rows, columns, dtype=F32):
        return jax.ShapeDtypeStruct((rows, columns), dtype)

    size0, size1 = n0 * chunks, n1 * chunks
    slab = pl.pallas_call(
        functools.partial(slab_kernel, strides[0]),
        out_shape=shape(16, cols),
        in_specs=[hbm],
        out_specs=vmem,
        scratch_shapes=[pltpu.SemaphoreType.DMA((n0,))],
        compiler_params=limit(53),
        cost_estimate=cost(0, 200000),
        name="sample_slabs",
    )(record)
    own0 = pl.pallas_call(
        functools.partial(first_kernel, strides[0]),
        out_shape=shape(size0, LANES, BF16),
        in_specs=[vmem, vmem],
        out_specs=vmem,
        scratch_shapes=[pltpu.VMEM((16 * chunks, LANES), F32)],
        compiler_params=limit(8),
        cost_estimate=cost(0, 200000),
        name="first_samples",
    )(phases[None], slab)

    z8, z12, z4 = [swap(own0, bit) for bit in (8, 12, 4)]
    others = [z4, z12, z8]
    rounded, sel, own = pl.pallas_call(
        functools.partial(local_kernel, strides),
        out_shape=(
            shape(steps, cols, BF16), shape(size_m, cols, BF16), shape(size0 + size1, LANES, BF16)
        ),
        in_specs=[vmem] * 3,
        out_specs=(vmem,) * 3,
        scratch_shapes=[pltpu.VMEM((16 * chunks, LANES), F32)],
        compiler_params=limit(12),
        cost_estimate=cost(1000, 1000),
        name="local_samples",
    )(phases[None], record, own0)
    side, near = swap(own, 2), swap(own, 1)
    others, rounded, sel = lax.optimization_barrier((others, rounded, sel))
    far = jnp.concatenate(others, axis=0)
    side_far = swap(far, 2)
    far, phases_then = lax.optimization_barrier((far, phases))
    modes = pl.pallas_call(
        functools.partial(modes_kernel, strides),
        out_shape=(
            jax.ShapeDtypeStruct((3, modes_r, size_m), F32),
            shape(3 * modes_r, 3 * size_m),
            shape(modes_r, steps),
        ),
        in_specs=[vmem, hbm, vmem],
        out_specs=(vmem,) * 3,
        scratch_shapes=[
            pltpu.VMEM((3, size_m, size_m), F32),
            pltpu.SemaphoreType.DMA((3,)),
        ],
        compiler_params=limit(4),
        cost_estimate=cost(1000, 1000),
        name="chosen_modes",
    )(phases_then[None], mode_basis, slow_picks)

    side, modes = lax.optimization_barrier((side, modes))
    bt, bd, bx = modes
    near_far, next_side = swap(far, 1), swap(side, 1)
    own_then, side_far, near_far = lax.optimization_barrier((own, side_far, near_far))
    next_far = swap(side_far, 1)
    near = [own_then, side, near, next_side]
    first = 2 * size_m // 3 // 16 * 16
    gram, early = pl.pallas_call(
        functools.partial(gram_kernel, points, size0),
        out_shape=(shape(size_m, size_m), shape(first + 2 * size_m, cols, BF16)),
        in_specs=[vmem] * 8,
        out_specs=(vmem, vmem),
        scratch_shapes=[
            pltpu.VMEM((size_m * chunks, LANES), F32), pltpu.VMEM((size_m, cols), BF16)
        ],
        compiler_params=limit(8),
        cost_estimate=cost(1000, 1000),
        name="level_1_gram",
    )(sel, *near, far, side_far, near_far)
    next_far, gram, early = lax.optimization_barrier((next_far, gram, early))
    w, last = pl.pallas_call(
        functools.partial(cross_kernel, points, size0),
        out_shape=(
            shape(3 * modes_r, steps + 2 * modes_r), shape(size_m - first, cols, BF16)
        ),
        in_specs=[vmem] * 8,
        out_specs=(vmem, vmem),
        scratch_shapes=[pltpu.VMEM(((size_m - first) * chunks, LANES), F32)],
        compiler_params=limit(8),
        cost_estimate=cost(1000000000, 3000000),
        name="cross_products",
    )(rounded, early, gram, bd, bx, near_far, next_side, next_far)

    distance = 1
    other = jnp.zeros_like(w)
    while distance < spaces:
        other = lax.ppermute(w, "space", [(i, i ^ distance) for i in range(spaces)])
        distance *= 2
        if distance < spaces:
            w = w + other

    return pl.pallas_call(
        solve_kernel,
        out_shape=shape(steps, cols),
        in_specs=[vmem] * 6,
        out_specs=hbm,
        scratch_shapes=[
            pltpu.VMEM((steps, cols), F32),
            pltpu.VMEM((3 * modes_r, cols), BF16),
            pltpu.SemaphoreType.DMA((8,)),
        ],
        compiler_params=limit(16),
        cost_estimate=cost(1000000000, 9000000),
        name="remove_slow",
    )(w, other, bt, record, early, last)


def solution(mesh):
    in_specs = (P("tm", "space"), P(), P(), P())
    out_specs = P("tm", "space")
    return jax.shard_map(body, mesh=mesh, in_specs=in_specs, out_specs=out_specs, check_vma=False)
```

```python
import functools

import jax
import jax.numpy as jnp
from jax import lax
from jax.experimental import pallas as pl
from jax.experimental.pallas import tpu as pltpu
from jax.sharding import PartitionSpec as P

EPS = 1e-05
HI = lax.Precision.HIGHEST
F32 = jnp.float32
BF16 = jnp.bfloat16
LANES = 128
ROWS = 8
MIB = 1024 * 1024


def dot_nn(a, b, precision=None):
    return lax.dot_general(
        a, b, (((1,), (0,)), ((), ())), precision=precision, preferred_element_type=F32
    )


def dot_nt(a, b, precision=None):
    return lax.dot_general(
        a, b, (((1,), (1,)), ((), ())), precision=precision, preferred_element_type=F32
    )


def dot_tn(a, b, precision=None):
    return lax.dot_general(
        a, b, (((0,), (0,)), ((), ())), precision=precision, preferred_element_type=F32
    )


def split2(x):
    high = x.astype(BF16)
    return high, (x - high.astype(F32)).astype(BF16)


def split3(x):
    high = x.astype(BF16)
    rest = x - high.astype(F32)
    middle = rest.astype(BF16)
    return high, middle, (rest - middle.astype(F32)).astype(BF16)


def dot_six(a, b):
    m = a.shape[0]
    a0, a1, a2 = split3(a)
    b0, b1, b2 = split3(b)
    p0 = dot_nn(jnp.concatenate([a0, a1, a2], axis=0), b0)
    p1 = dot_nn(jnp.concatenate([a0, a1], axis=0), b1)
    p2 = dot_nn(a0, b2)
    small = (p0[2 * m:3 * m] + p1[m:2 * m]) + p2
    return (small + (p0[m:2 * m] + p1[0:m])) + p0[0:m]


def iota(shape, axis):
    return lax.broadcasted_iota(jnp.int32, shape, axis)


def pick_phase(phases_ref, window, stride):
    phases = phases_ref[...]
    here = iota(phases.shape, 1) == window
    return lax.rem(jnp.sum(jnp.where(here, phases, 0), axis=1, keepdims=True), stride)


def slab_kernel(stride0, x_hbm, slab_ref, sems):
    size = 4
    copies = [
        pltpu.make_async_copy(
            x_hbm.at[pl.ds(stride0 * i, size), :], slab_ref.at[pl.ds(size * i, size), :], sems.at[i]
        )
        for i in range(sems.shape[0])
    ]
    for copy in copies:
        copy.start(priority=1)
    rows, cols = slab_ref.shape
    used = size * sems.shape[0]
    slab_ref[used:rows] = jnp.zeros((rows - used, cols), F32)
    for copy in copies:
        copy.wait()


def first_kernel(stride0, phases_ref, slab_ref, out_ref, wide_ref):
    rows, cols = slab_ref.shape
    chunks = cols // LANES
    count = out_ref.shape[0] // chunks
    held = wide_ref.shape[0] // chunks
    off = pick_phase(phases_ref, 0, stride0)
    line, place = iota((held, rows), 0), iota((held, rows), 1)
    pick = ((place == 4 * line + off) & (line < count)).astype(BF16)
    wide = 512
    for p in range(cols // wide):
        got = dot_nn(pick, slab_ref[:, p * wide:(p + 1) * wide].astype(BF16))
        for c in range(wide // LANES):
            wide_ref[pl.ds(p * wide // LANES + c, held, stride=chunks), :] = got[
                :, c * LANES:(c + 1) * LANES
            ]
    out_ref[...] = wide_ref[0:count * chunks].astype(BF16)


def local_kernel(strides, phases_ref, x_ref, own0_ref, round_ref, sel_ref, own_ref, wide_ref):
    pos = lax.axis_index("tm")
    steps, cols = x_ref.shape
    chunks = cols // LANES
    size_m = sel_ref.shape[0]
    size0 = own0_ref.shape[0]
    n1 = steps // strides[1]
    held = wide_ref.shape[0] // chunks
    off1 = pick_phase(phases_ref, 1 + lax.div(pos, 4), strides[1])
    off2 = pick_phase(phases_ref, 5 + pos, strides[2])
    line, place = iota((size_m + held, steps), 0), iota((size_m + held, steps), 1)
    second = line >= size_m
    line = jnp.where(second, line - size_m, line)
    target = jnp.where(second, line * strides[1] + off1, line * strides[2] + off2)
    pick = ((place == target) & jnp.logical_not(second & (line >= n1))).astype(BF16)
    parts = 8
    wide = cols // parts
    for p in range(parts):
        at = slice(p * wide, (p + 1) * wide)
        rounded = x_ref[:, at].astype(BF16)
        round_ref[:, at] = rounded
        got = dot_nn(pick, rounded)
        sel_ref[:, at] = got[0:size_m].astype(BF16)
        for c in range(wide // LANES):
            wide_ref[pl.ds(p * wide // LANES + c, held, stride=chunks), :] = got[
                size_m:size_m + held, c * LANES:(c + 1) * LANES
            ]
    own_ref[0:size0] = own0_ref[...]
    own_ref[size0:size0 + n1 * chunks] = wide_ref[0:n1 * chunks].astype(BF16)


def modes_kernel(strides, phases_ref, basis_hbm, picks_ref, bt_ref, bd_ref, bx_ref, basis_ref, sems):
    pos = lax.axis_index("tm")
    modes_r, steps = bx_ref.shape
    size_m = basis_ref.shape[1]
    n0, n1 = steps // strides[0], steps // strides[1]
    windows = [0, 1 + lax.div(pos, 4), 5 + pos]
    copies = [
        pltpu.make_async_copy(basis_hbm.at[windows[level]], basis_ref.at[level], sems.at[level])
        for level in range(3)
    ]
    for copy in copies:
        copy.start()
    lane = iota((1, size_m), 1)

    def placed(width, flips, base):
        order = jnp.zeros((1, size_m), jnp.int32)
        for b, flip in enumerate(flips):
            inside = (lane >= b * width) & (lane < (b + 1) * width)
            order = jnp.where(inside, (base ^ flip) * width + lane - b * width, order)
        return order

    flips0 = [(b // 8) + (b // 4 % 2) * 2 + (0, 4, 12, 8)[b % 4] for b in range(16)]
    flips1 = [(b // 2) + (b % 2) * 2 for b in range(4)]
    orders = [placed(n0, flips0, pos), placed(n1, flips1, lax.rem(pos, 4)), lane]
    for copy in copies:
        copy.wait()
    for level in range(3):
        picks = picks_ref[pl.ds(windows[level], 1), :]
        onehot = (iota((size_m, modes_r), 0) == picks).astype(F32)
        chosen = dot_nn(basis_ref[level], onehot, HI)
        shuffle = (iota((size_m, size_m), 0) == orders[level]).astype(F32)
        bt_ref[level] = dot_tn(chosen, shuffle, HI)
    off2 = pick_phase(phases_ref, windows[2], strides[2])
    place = (iota((size_m, steps), 1) == iota((size_m, steps), 0) * strides[2] + off2)
    bx_ref[...] = dot_nn(bt_ref[2], place.astype(F32), HI)
    bd_ref[...] = jnp.zeros(bd_ref.shape, F32)
    for level in range(3):
        bd_ref[level * modes_r:(level + 1) * modes_r, level * size_m:(level + 1) * size_m] = bt_ref[level]


def unpack(pieces, wide_ref, s_ref, count):
    at = 0
    for piece, first, last in pieces:
        wide_ref[at:at + last - first] = piece[first:last].astype(F32)
        at += last - first
    chunks = s_ref.shape[1] // LANES
    for c in range(chunks):
        s_ref[0:count, c * LANES:(c + 1) * LANES] = wide_ref[
            pl.ds(c, count, stride=chunks), :
        ].astype(BF16)


def gram_kernel(points, size0, sel_ref, *refs):
    near, far, (gram_ref, s_ref, wide_ref, gather_ref) = refs[:4], refs[4:7], refs[7:]
    count, cols = sel_ref.shape
    first = s_ref.shape[0] - 2 * count
    unpack([(piece, size0, piece.shape[0]) for piece in near], wide_ref, gather_ref, count)
    s = gather_ref[0:count]
    gram_ref[...] = dot_nt(s, s) * (1.0 / points)
    s_ref[first:first + count] = s
    s_ref[first + count:first + 2 * count] = sel_ref[...]
    pieces, left = [], first * (cols // LANES)
    for i in range(3):
        for piece, size in ((near[i], size0), (far[i], far[i].shape[0])):
            take = min(size, left)
            if take:
                pieces.append((piece, 0, take))
                left -= take
    unpack(pieces, wide_ref, s_ref, first)


def cross_kernel(points, size0, round_ref, early_ref, gram_ref, bd_ref, bx_ref, far2_ref, near3_ref, far3_ref,
                 w_ref, s_ref, wide_ref):
    r, steps = bx_ref.shape
    count = gram_ref.shape[0]
    first = early_ref.shape[0] - 2 * count
    chunks = early_ref.shape[1] // LANES
    done = (first - count // 2) * chunks - size0
    size = far2_ref.shape[0]
    unpack([(far2_ref, done, size), (near3_ref, 0, size0), (far3_ref, 0, size)], wide_ref, s_ref, count - first)
    s0 = jnp.concatenate([early_ref[0:first], s_ref[...]], axis=0)
    s = jnp.concatenate([s0, early_ref[first:]], axis=0)
    cross = dot_nt(s, jnp.concatenate([round_ref[...], s0], axis=0)) * (1.0 / points)
    b0, b1 = bd_ref[0:r, 0:count], bd_ref[r:2 * r, count:2 * count]
    wx = dot_six(bd_ref[...], cross[:, 0:steps])
    g0 = dot_nn(bd_ref[0:2 * r, 0:2 * count], cross[0:2 * count, steps:steps + count], HI)
    g1 = dot_nn(b1, gram_ref[...], HI)
    wy = dot_nt(b0, g0, HI)
    at1, at2 = steps, steps + r
    w_ref[:, 0:steps] = wx
    w_ref[0:r, at1:at1 + r] = wy[:, r:2 * r]
    w_ref[r:2 * r, at1:at1 + r] = dot_nt(g1, b1, HI)
    w_ref[2 * r:3 * r, at1:at1 + r] = wy[:, 0:r]
    w_ref[:, at2:at2 + r] = dot_nt(wx, bx_ref[...], HI)


def inverse4(p):
    a, b, d = p[0][0], p[1][0], p[1][1]
    e, f, g, h = p[2][0], p[3][0], p[2][1], p[3][1]
    u, v, w = p[2][2], p[3][2], p[3][3]
    i = 1.0 / (a * d - b * b)
    t00, t01 = (d * e - b * g) * i, (d * f - b * h) * i
    t10, t11 = (a * g - b * e) * i, (a * h - b * f) * i
    s00 = u - (e * t00 + g * t10)
    s01 = v - (e * t01 + g * t11)
    s11 = w - (f * t01 + h * t11)
    j = 1.0 / (s00 * s11 - s01 * s01)
    m22, m23, m33 = s11 * j, -(s01 * j), s00 * j
    y00, y01 = t00 * m22 + t01 * m23, t00 * m23 + t01 * m33
    y10, y11 = t10 * m22 + t11 * m23, t10 * m23 + t11 * m33
    m00 = d * i + (y00 * t00 + y01 * t01)
    m01 = (y00 * t10 + y01 * t11) - b * i
    m11 = a * i + (y10 * t10 + y11 * t11)
    return [
        [m00, m01, -y00, -y01],
        [m01, m11, -y10, -y11],
        [-y00, -y10, m22, m23],
        [-y01, -y11, m23, m33],
    ]


def along_lanes(tile, lane):
    return jnp.broadcast_to(tile[:, lane:lane + 1], tile.shape)


def along_rows(tile, row):
    return jnp.broadcast_to(tile[row:row + 1, :], tile.shape)


def sum4(terms):
    return (terms[0] + terms[1]) + (terms[2] + terms[3])


def eliminate(tiles, at, base, beside=None):
    groups, width = len(tiles), len(tiles[0])
    sub = iota((ROWS, LANES), 0)
    four = range(4)
    tiles = [list(row) for row in tiles]
    cols = [[along_lanes(tiles[g][at], base + j) for g in range(groups)] for j in four]
    pivot = [[along_rows(cols[j][0], i) for j in range(i + 1)] for i in four]
    for k in range(0, groups * ROWS, 4):
        home, first = k // ROWS, k % ROWS
        m = inverse4(pivot)
        if beside is not None:
            beside(k // 4)
        if k + 4 < groups * ROWS:
            then, start = (k + 4) // ROWS, (k + 4) % ROWS
            left = [[along_rows(cols[j][then], start + i) for j in four] for i in four]
            diag = [along_lanes(tiles[then][at], base + k + 4 + j) for j in four]
            diag = [[along_rows(diag[j], start + i) for j in range(i + 1)] for i in four]
            mixed = [[sum4([m[a][j] * left[i][j] for j in four]) for i in four] for a in four]
            pivot = [
                [diag[i][j] - sum4([left[i][a] * mixed[a][j] for a in four]) for j in range(i + 1)]
                for i in four
            ]
        rows = [[along_rows(tiles[home][t], first + i) for t in range(width)] for i in four]
        news = [
            [sum4([m[i][j] * rows[j][t] for j in four]) for t in range(width)] for i in four
        ]
        for g in range(groups):
            for t in range(width):
                tile = tiles[g][t] - sum4([cols[j][g] * news[j][t] for j in four])
                if g == home:
                    for i in four:
                        tile = jnp.where(sub == first + i, news[i][t], tile)
                tiles[g][t] = tile
        if k + 4 < groups * ROWS:
            cols = [[along_lanes(tiles[g][at], base + k + 4 + j) for g in range(groups)] for j in four]
    return tiles


def to_tiles(value):
    return [
        [
            value[g * ROWS:(g + 1) * ROWS, t * LANES:(t + 1) * LANES]
            for t in range(value.shape[1] // LANES)
        ]
        for g in range(value.shape[0] // ROWS)
    ]


def from_tiles(tiles):
    return jnp.concatenate([jnp.concatenate(row, axis=1) for row in tiles], axis=0)


def solve_kernel(w_ref, got_ref, bt_ref, x_ref, early_ref, last_ref, out_hbm, out_ref, z_ref, out_sems):
    r = bt_ref.shape[1]
    count = bt_ref.shape[2]
    steps, cols = x_ref.shape
    first = count - last_ref.shape[0]
    w = w_ref[...] + got_ref[...]
    lanes = w.shape[1]
    b0, b1, b2 = bt_ref[0], bt_ref[1], bt_ref[2]

    def eye_at(base, width):
        return jnp.where(iota((r, width), 0) + base == iota((r, width), 1), EPS, 0.0)

    at1, at2 = steps, steps + r
    assert at1 // LANES == (at2 + r - 1) // LANES
    a0 = w[0:r]
    tile1, lane1 = at1 // LANES, at1 % LANES
    tile2, lane2 = at2 // LANES, at2 % LANES
    k0 = w[2 * r:3 * r] + eye_at(at1, lanes)
    solved = eliminate(
        to_tiles(jnp.concatenate([a0, k0[:, tile1 * LANES:(tile1 + 1) * LANES]], axis=1)),
        lanes // LANES, lane1,
    )
    v0 = from_tiles([row[0:lanes // LANES] for row in solved])
    t0 = a0 + EPS * v0
    a1 = w[r:2 * r] - dot_tn(v0[:, at1:at1 + r], t0, HI)
    part2 = w[2 * r:3 * r] - dot_tn(v0[:, at2:at2 + r], t0, HI)
    v1 = from_tiles(eliminate(to_tiles(a1 + eye_at(at1, lanes)), tile1, lane1))
    t1 = a1 + EPS * v1
    a2 = part2 - dot_tn(v1[:, at2:at2 + r], t1, HI)
    v0 = v0 - dot_nn(v0[:, at1:at1 + r], v1, HI)
    early = jnp.concatenate(
        [dot_tn(v0[:, 0:steps], b0, HI), dot_tn(v1[:, 0:steps], b1, HI)], axis=1
    )
    early = jnp.concatenate(split2(early), axis=0)
    turn = jnp.concatenate(
        [-dot_tn(v0[:, at2:at2 + r], b0, HI), -dot_tn(v1[:, at2:at2 + r], b1, HI), b2], axis=1
    )
    turn = jnp.concatenate(split2(turn), axis=0)
    parts = r // 4
    wide = cols // parts

    def beside(p):
        at = slice(p * wide, (p + 1) * wide)
        s = jnp.concatenate(
            [early_ref[0:first, at], last_ref[:, at], early_ref[first:, at]], axis=0
        )
        slow = dot_nn(early, s[0:2 * count])
        out_ref[:, at] = x_ref[:, at] - (slow[0:steps] + slow[steps:2 * steps])
        both = dot_nn(turn, s)
        high, low = split2(both[0:r] + both[r:2 * r])
        z_ref[0:r, at] = high
        z_ref[r:2 * r, at] = high
        z_ref[2 * r:3 * r, at] = low

    v2 = from_tiles(eliminate(to_tiles(a2 + eye_at(at2, lanes)), tile2, lane2, beside))
    high = v2[:, 0:steps].astype(BF16).astype(F32)
    late = jnp.concatenate([high, v2[:, 0:steps] - high, high], axis=0).T.astype(BF16)
    copies = []
    parts = out_sems.shape[0]
    wide = cols // parts
    for p in range(parts):
        at = slice(p * wide, (p + 1) * wide)
        out_ref[:, at] = out_ref[:, at] - dot_nn(late, z_ref[:, at])
        copy = pltpu.make_async_copy(out_ref.at[:, at], out_hbm.at[:, at], out_sems.at[p])
        copy.start()
        copies.append(copy)
    for copy in copies:
        copy.wait()


def body(record, mode_basis, slow_picks, phases):
    steps, cols = record.shape
    size_m = mode_basis.shape[1]
    modes_r = slow_picks.shape[1]
    groups = lax.axis_size("tm")
    spaces = lax.axis_size("space")
    assert groups == 16 and cols % 512 == 0
    points = cols * spaces
    chunks = cols // LANES
    strides = tuple(steps * groups // (4**level * size_m) for level in range(3))
    n0, n1 = steps // strides[0], steps // strides[1]
    vmem = pl.BlockSpec(memory_space=pltpu.VMEM)
    hbm = pl.BlockSpec(memory_space=pltpu.HBM)

    def cost(flops, size):
        return pl.CostEstimate(flops=flops, bytes_accessed=size, transcendentals=0)

    def limit(size):
        return pltpu.CompilerParams(vmem_limit_bytes=size * MIB)

    def swap(value, bit):
        return lax.ppermute(value, "tm", [(i, i ^ bit) for i in range(groups)])

    def shape(rows, columns, dtype=F32):
        return jax.ShapeDtypeStruct((rows, columns), dtype)

    size0, size1 = n0 * chunks, n1 * chunks
    slab = pl.pallas_call(
        functools.partial(slab_kernel, strides[0]),
        out_shape=shape(16, cols),
        in_specs=[hbm],
        out_specs=vmem,
        scratch_shapes=[pltpu.SemaphoreType.DMA((n0,))],
        compiler_params=limit(53),
        cost_estimate=cost(0, 200000),
        name="sample_slabs",
    )(record)
    own0 = pl.pallas_call(
        functools.partial(first_kernel, strides[0]),
        out_shape=shape(size0, LANES, BF16),
        in_specs=[vmem, vmem],
        out_specs=vmem,
        scratch_shapes=[pltpu.VMEM((16 * chunks, LANES), F32)],
        compiler_params=limit(8),
        cost_estimate=cost(0, 200000),
        name="first_samples",
    )(phases[None], slab)

    z8, z12, z4 = [swap(own0, bit) for bit in (8, 12, 4)]
    others = [z4, z12, z8]
    rounded, sel, own = pl.pallas_call(
        functools.partial(local_kernel, strides),
        out_shape=(
            shape(steps, cols, BF16), shape(size_m, cols, BF16), shape(size0 + size1, LANES, BF16)
        ),
        in_specs=[vmem] * 3,
        out_specs=(vmem,) * 3,
        scratch_shapes=[pltpu.VMEM((16 * chunks, LANES), F32)],
        compiler_params=limit(12),
        cost_estimate=cost(1000, 1000),
        name="local_samples",
    )(phases[None], record, own0)
    side, near = swap(own, 2), swap(own, 1)
    others, rounded, sel = lax.optimization_barrier((others, rounded, sel))
    far = jnp.concatenate(others, axis=0)
    side_far = swap(far, 2)
    far, phases_then = lax.optimization_barrier((far, phases))
    modes = pl.pallas_call(
        functools.partial(modes_kernel, strides),
        out_shape=(
            jax.ShapeDtypeStruct((3, modes_r, size_m), F32),
            shape(3 * modes_r, 3 * size_m),
            shape(modes_r, steps),
        ),
        in_specs=[vmem, hbm, vmem],
        out_specs=(vmem,) * 3,
        scratch_shapes=[
            pltpu.VMEM((3, size_m, size_m), F32),
            pltpu.SemaphoreType.DMA((3,)),
        ],
        compiler_params=limit(4),
        cost_estimate=cost(1000, 1000),
        name="chosen_modes",
    )(phases_then[None], mode_basis, slow_picks)

    side, modes = lax.optimization_barrier((side, modes))
    bt, bd, bx = modes
    near_far, next_side = swap(far, 1), swap(side, 1)
    own_then, side_far, near_far = lax.optimization_barrier((own, side_far, near_far))
    next_far = swap(side_far, 1)
    near = [own_then, side, near, next_side]
    first = 2 * size_m // 3 // 16 * 16
    gram, early = pl.pallas_call(
        functools.partial(gram_kernel, points, size0),
        out_shape=(shape(size_m, size_m), shape(first + 2 * size_m, cols, BF16)),
        in_specs=[vmem] * 8,
        out_specs=(vmem, vmem),
        scratch_shapes=[
            pltpu.VMEM((size_m * chunks, LANES), F32), pltpu.VMEM((size_m, cols), BF16)
        ],
        compiler_params=limit(8),
        cost_estimate=cost(1000, 1000),
        name="level_1_gram",
    )(sel, *near, far, side_far, near_far)
    next_far, gram, early = lax.optimization_barrier((next_far, gram, early))
    w, last = pl.pallas_call(
        functools.partial(cross_kernel, points, size0),
        out_shape=(
            shape(3 * modes_r, steps + 2 * modes_r), shape(size_m - first, cols, BF16)
        ),
        in_specs=[vmem] * 8,
        out_specs=(vmem, vmem),
        scratch_shapes=[pltpu.VMEM(((size_m - first) * chunks, LANES), F32)],
        compiler_params=limit(8),
        cost_estimate=cost(1000000000, 3000000),
        name="cross_products",
    )(rounded, early, gram, bd, bx, near_far, next_side, next_far)

    distance = 1
    other = jnp.zeros_like(w)
    while distance < spaces:
        other = lax.ppermute(w, "space", [(i, i ^ distance) for i in range(spaces)])
        distance *= 2
        if distance < spaces:
            w = w + other

    return pl.pallas_call(
        solve_kernel,
        out_shape=shape(steps, cols),
        in_specs=[vmem] * 6,
        out_specs=hbm,
        scratch_shapes=[
            pltpu.VMEM((steps, cols), F32),
            pltpu.VMEM((3 * modes_r, cols), BF16),
            pltpu.SemaphoreType.DMA((8,)),
        ],
        compiler_params=limit(16),
        cost_estimate=cost(1000000000, 9000000),
        name="remove_slow",
    )(w, other, bt, record, early, last)


def solution(mesh):
    in_specs = (P("tm", "space"), P(), P(), P())
    out_specs = P("tm", "space")
    return jax.shard_map(body, mesh=mesh, in_specs=in_specs, out_specs=out_specs, check_vma=False)
```
